128 devices in a mesh: role: 2 (over y_hi), tile: 64 (over y_lo, x, z, core).
Axes of the slice: x: 4, y: 4 (y_hi: 2, y_lo: 2; y = y_hi * 2 + y_lo), z: 4, core: 2. Of those that a mesh axis runs over, the one named last changes fastest.
Arguments:
- fields_pair: float32 [2, 512, 65536], P('role', None, 'tile'), may hold values from 0 to 1
- velocity: float32 [65536], P('tile'), may hold values from -0.5 to 0.5
- growth: float32 [65536], P('tile'), may hold values from 0.05 to 0.5
- features: bfloat16 [512, 1024], replicated, may hold values from -6 to 6
- assignment: int32 [512], replicated, may hold values from 0 to 511, each once
- out_pair: float32 [2, 1024, 65536], P('role', None, 'tile'), may hold values from -0.1875 to 0.1875
- hidden_pair: float32 [2, 5, 1024, 1024], P('role', None, 'tile'), may hold values from -0.1875 to 0.1875
Outputs:
- fields_next: float32 [2, 512, 65536], P('role', None, 'tile')
- out_next: float32 [2, 1024, 65536], P('role', None, 'tile')
- hidden_next: float32 [2, 5, 1024, 1024], P('role', None, 'tile')
The draws below stay inside these ranges and needn't reach their ends.
Inputs may be any that keep to these rules, and one draw needn't show every extreme that they name: `assignment`: a permutation of the 512 members.
All inputs are finite; a program needn't handle non-finite values.
Results may differ from the reference program's by a relative error of at most 0.0022.
The reference program's roundings to bfloat16 on the way (of `residual`) count: a program that leaves them out, or rounds other values in their place, can miss the bound.
Values may be sent and summed in bfloat16 or wider, within the bound.
No kernel may reach another device: no remote copies, remote signals or barrier semaphores. Data moves between devices by JAX's collectives and lax.ppermute only.
A program may use at most 192 MiB of HBM per device.

```python
import math
import jax
import jax.numpy as jnp

BATCH = 512
HID = 1024
LAYERS = 5
SLAB = 65536


def block_levels(stream_key, shape, split, low, high):
    def one(dim, parts):
        steps = jax.random.uniform(jax.random.fold_in(jax.random.fold_in(stream_key, 6), dim), (parts,), jnp.float32, low / len(split), high / len(split))
        return jnp.repeat(jnp.exp(steps), shape[dim] // parts).reshape((-1,) + (1,) * (len(shape) - dim - 1))

    loudness = one(*split[0])
    for cut in split[1:]:
        loudness = loudness * one(*cut)
    return loudness


def bell_draw(own_key, dims, width, bound, split=(), kind=jnp.bfloat16):
    drawn = width * jax.random.normal(own_key, dims, jnp.float32)
    if split:
        drawn = drawn * block_levels(own_key, dims, split, -0.22, 0.18)
    return jnp.clip(drawn, -bound, bound).astype(kind)


def setup_inputs(seed: int = 0) -> dict:
    streams_of = jax.random.split(jax.random.key(seed), 8)
    return {
        "fields_pair": jnp.clip(1.0 * jax.random.uniform(streams_of[0], (2, BATCH, SLAB), jnp.float32) ** block_levels(streams_of[0], (2, BATCH, SLAB), ((0, 2), (2, 64)), -0.2, 0.2), 0.0, 1.0),
        "velocity": jnp.clip(jax.random.uniform(streams_of[1], (SLAB,), jnp.float32, -0.5, 0.5) * block_levels(streams_of[1], (SLAB,), ((0, 64),), -0.4, 0.0), -0.5, 0.5),
        "growth": jnp.clip(jnp.exp(math.log(0.5) - 2.3025851 * jax.random.uniform(streams_of[2], (SLAB,), jnp.float32) ** block_levels(streams_of[2], (SLAB,), ((0, 64),), -0.2, 0.2)), 0.05, 0.5),
        "features": bell_draw(streams_of[3], (BATCH, HID), 1.0, 6.0),
        "assignment": jax.random.permutation(streams_of[4], BATCH).astype(jnp.int32),
        "out_pair": bell_draw(streams_of[5], (2, HID, SLAB), HID ** -0.5, 0.1875, ((0, 2), (2, 64)), jnp.float32),
        "hidden_pair": bell_draw(streams_of[6], (2, LAYERS, HID, HID), HID ** -0.5, 0.1875, ((0, 2), (2, 64)), jnp.float32),
    }


def silu_slope(values):
    logistic = jax.nn.sigmoid(values)
    return logistic * (1.0 + values * (1.0 - logistic))


def reference(fields_pair, velocity, growth, features, assignment, out_pair, hidden_pair):
    current = fields_pair[0]
    target = fields_pair[1]
    forward_cell = jnp.roll(current, -1, axis=1)
    outflow = jnp.maximum(velocity, 0.0) * current + jnp.minimum(velocity, 0.0) * forward_cell
    carried = current - outflow + jnp.roll(outflow, 1, axis=1)
    advanced = carried + growth * carried * (1.0 - carried)
    next_batch = jnp.take(advanced, assignment, axis=0)
    weights = hidden_pair[1]
    momenta = hidden_pair[0]
    inputs = []
    summed_list = []
    activation = features
    for layer_index in range(LAYERS):
        inputs.append(activation)
        summed = jnp.dot(activation, weights[layer_index].astype(jnp.bfloat16), preferred_element_type=jnp.float32)
        summed_list.append(summed)
        activation = jax.nn.silu(summed).astype(jnp.bfloat16)
    out_narrow = out_pair[1].astype(jnp.bfloat16)
    predicted = jnp.dot(activation, out_narrow, preferred_element_type=jnp.float32)
    residual = ((predicted - target) / BATCH).astype(jnp.bfloat16)
    grad_out = jnp.dot(activation.T, residual, preferred_element_type=jnp.float32)
    upstream = jnp.dot(residual, out_narrow.T, preferred_element_type=jnp.float32)
    gradients = []
    for layer_index in reversed(range(LAYERS)):
        slope = (upstream * silu_slope(summed_list[layer_index])).astype(jnp.bfloat16)
        gradients.append(jnp.dot(inputs[layer_index].T, slope, preferred_element_type=jnp.float32))
        if layer_index > 0:
            upstream = jnp.dot(slope, weights[layer_index].astype(jnp.bfloat16).T, preferred_element_type=jnp.float32)
    grad_hidden = jnp.stack(gradients[::-1])
    momentum_out = 0.9 * out_pair[0] + grad_out
    weight_out = out_pair[1] - 0.1 * momentum_out
    momentum_hidden = 0.9 * momenta + grad_hidden
    weight_hidden = weights - 0.1 * momentum_hidden
    return (jnp.stack([advanced, next_batch]), jnp.stack([momentum_out, weight_out]), jnp.stack([momentum_hidden, weight_hidden]))
```

```python
import itertools

import jax
import jax.numpy as jnp
from jax import lax
from jax.experimental import pallas as pl
from jax.experimental.pallas import tpu as pltpu
from jax.sharding import Mesh
from jax.sharding import PartitionSpec as P

BATCH = 512
LAYERS = 5
TILE = ("tile_0", "tile_1", "tile_2", "tile_3")
CHIPS = ("tile_0", "tile_1", "tile_2")
ALL = ("role", *TILE)

momentum_decay = 0.9
step_size = 0.1


def to_trainer(value):
    return lax.ppermute(value, "role", [(0, 1)])


def to_solver(value):
    return lax.ppermute(value, "role", [(1, 0)])


def swapped(value, axis):
    return lax.ppermute(value, axis, [(0, 1), (1, 0)])


def from_everyone(value, axes):
    copies = jnp.broadcast_to(value, (lax.axis_size(axes), *value.shape))
    return lax.all_to_all(copies, axes, split_axis=0, concat_axis=0, tiled=True)


def ordered(mine, other, place, axis):
    return jnp.where(
        place == 0, jnp.stack([mine, other], axis), jnp.stack([other, mine], axis)
    )


def advance(fields, before, after, velocity, growth):
    states = jnp.concatenate([before[:BATCH, -1:], fields, after[:, :1]], axis=1)
    speeds = jnp.concatenate([before[BATCH, -1:], velocity])
    outflow = (
        jnp.maximum(speeds, 0.0) * states[:, :-1] + jnp.minimum(speeds, 0.0) * states[:, 1:]
    )
    carried = fields - outflow[:, 1:] + outflow[:, :-1]
    return carried + growth * carried * (1.0 - carried)


def along(value, plane_axis, step):
    sizes = [lax.axis_size(name) for name in ALL]
    pairs = []
    for role, pair, x, z, core in itertools.product(*map(range, sizes)):
        if role == 0:
            continue
        to_x, to_z = (x, (z + step) % sizes[3])
        if (core == 0) == (plane_axis == 0):
            to_x, to_z = ((x + step) % sizes[2], z)
        pairs.append((flat(sizes, (role, pair, x, z, core)), flat(sizes, (role, pair, to_x, to_z, core))))
    return lax.ppermute(value, ALL, pairs)


def flat(sizes, place):
    index = 0
    for size, coordinate in zip(sizes, place):
        index = index * size + coordinate
    return index


def trainers_swap(value, axis):
    sizes = [lax.axis_size(name) for name in ALL]
    which = ALL.index(axis)
    pairs = []
    for place in itertools.product(*map(range, sizes)):
        if place[0] == 1:
            other = list(place)
            other[which] = 1 - other[which]
            pairs.append((flat(sizes, place), flat(sizes, other)))
    return lax.ppermute(value, ALL, pairs)


def tied(value, *others):
    return lax.optimization_barrier((value, *others))[0]


UNITS = 16
COLUMNS = 256


def forward_kernel(*refs):
    pieces, features_ref = refs[:8], refs[8]
    inputs_ref, slopes_ref, weights_out, weights, first_sem, rest_sem, out_sem = refs[9:]
    pair = lax.axis_index("tile_0")
    x = lax.axis_index("tile_1")
    z = lax.axis_index("tile_2")
    core = lax.axis_index("tile_3")

    def start(first, layers, sem):
        for number, piece in enumerate(pieces):
            far = number % 4
            owner = core if number < 4 else 1 - core

            def step(index, carry, piece=piece, far=far, owner=owner):
                near = index // 2
                plane = lax.rem(pair + lax.rem(index, 2), 2)
                by_x = jnp.where(owner == 0, far, near)
                by_z = jnp.where(owner == 0, near, far)
                row = ((plane * 4 + lax.rem(x - by_x + 4, 4)) * 4 + lax.rem(z - by_z + 4, 4)) * 2 + owner
                row = pl.multiple_of(row * UNITS, UNITS)
                pltpu.make_async_copy(
                    piece.at[near, lax.rem(index, 2), pl.ds(first, layers)],
                    weights.at[pl.ds(first, layers), pl.ds(row, UNITS)],
                    sem,
                ).start()
                return carry

            lax.fori_loop(0, 8, step, 0)

    def finish(first, layers, sem):
        part = weights.at[pl.ds(first, layers)]
        pltpu.make_async_copy(part, part, sem).wait()

    start(0, 1, first_sem)
    start(1, LAYERS - 1, rest_sem)
    inputs_ref[0] = features_ref[...]
    finish(0, 1, first_sem)
    for layer in range(LAYERS):
        if layer == 1:
            finish(1, LAYERS - 1, rest_sem)
            keep = pltpu.make_async_copy(weights, weights_out, out_sem)
            keep.start()

        def block(index, carry, layer=layer):
            columns = pl.ds(pl.multiple_of(index * COLUMNS, COLUMNS), COLUMNS)
            total = jnp.dot(
                inputs_ref[layer], weights[layer, :, columns], preferred_element_type=jnp.float32
            )
            logistic = 1.0 / (1.0 + jnp.exp(-total))
            inputs_ref[layer + 1, :, columns] = (total * logistic).astype(jnp.bfloat16)
            slopes_ref[layer, :, columns] = logistic * (1.0 + total * (1.0 - logistic))
            return carry

        lax.fori_loop(0, weights.shape[2] // COLUMNS, block, 0)
    keep.wait()


def forward(pieces, features):
    rows, width = features.shape
    return pl.pallas_call(
        forward_kernel,
        out_shape=(
            jax.ShapeDtypeStruct((LAYERS + 1, rows, width), jnp.bfloat16),
            jax.ShapeDtypeStruct((LAYERS, rows, width), jnp.float32),
            jax.ShapeDtypeStruct((LAYERS, width, width), jnp.bfloat16),
        ),
        in_specs=[pl.BlockSpec(memory_space=pl.ANY)] * 8 + [pl.BlockSpec(memory_space=pltpu.VMEM)],
        out_specs=(
            pl.BlockSpec(memory_space=pltpu.VMEM),
            pl.BlockSpec(memory_space=pltpu.VMEM),
            pl.BlockSpec(memory_space=pl.ANY),
        ),
        scratch_shapes=[
            pltpu.VMEM((LAYERS, width, width), jnp.bfloat16),
            pltpu.SemaphoreType.DMA(()),
            pltpu.SemaphoreType.DMA(()),
            pltpu.SemaphoreType.DMA(()),
        ],
        compiler_params=pltpu.CompilerParams(vmem_limit_bytes=40 * 1024 * 1024),
        cost_estimate=pl.CostEstimate(
            flops=2 * LAYERS * rows * width * width,
            bytes_accessed=LAYERS * width * (4 * width + 6 * rows),
            transcendentals=LAYERS * rows * width,
        ),
    )(*pieces, features)


def body(fields_pair, velocity, growth, features, assignment, out_pair, hidden_pair):
    solver_side = lax.axis_index("role") == 0
    core = lax.axis_index("tile_3")
    chip = lax.axis_index(CHIPS)
    fields = fields_pair[0]
    own_out = out_pair[0]
    own_hidden = hidden_pair[0]
    units = own_hidden.shape[1]
    width = own_hidden.shape[2]
    half = BATCH // 2

    hidden_narrow = own_hidden.astype(jnp.bfloat16)
    out_narrow = own_out.astype(jnp.bfloat16)
    packed = jnp.concatenate([hidden_narrow.reshape(-1, width), out_narrow], axis=0)
    cut = 552
    edge = jnp.concatenate(
        [fields[:, -128:], jnp.broadcast_to(velocity[None, -128:], (8, 128))], axis=0
    )

    near = jnp.stack([hidden_narrow, trainers_swap(hidden_narrow, "tile_0")])
    momentum_a = to_trainer(packed[:cut])
    count = lax.axis_size(TILE)
    up = [(i, (i + 1) % count) for i in range(count)]
    down = [(j, i) for i, j in up]
    before = lax.ppermute(edge, TILE, up)
    after = lax.ppermute(fields[:, :128], TILE, down)
    stage = [near, *(along(near, 1, step) for step in (1, 2, 3))]
    stage, before, after, momentum_a = lax.optimization_barrier((stage, before, after, momentum_a))

    momentum_b = to_trainer(tied(packed[cut:], momentum_a))
    far = jnp.stack(stage)
    mine = [far, *(along(far, 0, step) for step in (1, 2, 3))]
    advanced = advance(fields, before, after, velocity, growth)
    carried = jnp.take(advanced.astype(jnp.bfloat16), assignment, axis=0)
    other = [trainers_swap(piece, "tile_3") for piece in mine]
    mine, other, carried, momentum_b = lax.optimization_barrier((mine, other, carried, momentum_b))
    next_batch = to_trainer(carried)
    inputs, slopes, weights = forward(
        [*mine, *other], lax.dynamic_slice_in_dim(features, core * half, half, 0)
    )
    activation = inputs[LAYERS]

    last = ordered(activation, swapped(activation, "tile_3"), core, 0).reshape(BATCH, width)
    predicted = jnp.dot(last, out_narrow, preferred_element_type=jnp.float32)
    residual = ((predicted - fields) / BATCH).astype(jnp.bfloat16)
    partial_grad = lax.dot_general(
        residual, out_narrow, (((1,), (1,)), ((), ())), preferred_element_type=jnp.float32
    )
    grad_out = lax.dot_general(
        last, residual, (((0,), (0,)), ((), ())), preferred_element_type=jnp.float32
    )
    grad_out_far = to_solver(grad_out.astype(jnp.bfloat16))

    kept = lax.dynamic_slice_in_dim(partial_grad, core * half, half, 0)
    given = lax.dynamic_slice_in_dim(partial_grad, (1 - core) * half, half, 0)
    chip_sum = kept + swapped(given, "tile_3")
    chips = lax.axis_size(CHIPS)
    rows = half // chips
    upstream = lax.all_to_all(
        chip_sum.reshape(chips, rows, width), CHIPS, split_axis=0, concat_axis=0, tiled=True
    ).sum(axis=0)
    upstream, next_batch = lax.optimization_barrier((upstream, next_batch))
    own_factor = lax.dynamic_slice_in_dim(slopes[LAYERS - 1], chip * rows, rows, 0)
    own_slope = (upstream * own_factor).astype(jnp.bfloat16)
    slope = from_everyone(own_slope, CHIPS).reshape(half, width)

    gradients = []
    for layer in reversed(range(LAYERS)):
        own_inputs = lax.dynamic_slice_in_dim(inputs[layer], chip * 2 * units, 2 * units, 1)
        gradients.append(
            lax.dot_general(
                own_inputs, slope, (((0,), (0,)), ((), ())), preferred_element_type=jnp.float32
            )
        )
        if layer > 0:
            upstream = lax.dot_general(
                slope, weights[layer], (((1,), (1,)), ((), ())), preferred_element_type=jnp.float32
            )
            slope = (upstream * slopes[layer - 1]).astype(jnp.bfloat16)
    pair_grad = jnp.stack(gradients[::-1])
    kept = lax.dynamic_slice_in_dim(pair_grad, core * units, units, 1)
    given = lax.dynamic_slice_in_dim(pair_grad, (1 - core) * units, units, 1)
    grad_hidden = kept + swapped(given, "tile_3")
    grad_hidden_far = to_solver(grad_hidden.astype(jnp.bfloat16))

    hidden_rows = packed.shape[0] - own_out.shape[0]
    momentum = jnp.concatenate([momentum_a, momentum_b], axis=0)
    other_hidden = momentum[:hidden_rows].reshape(own_hidden.shape).astype(jnp.float32)
    other_out = momentum[hidden_rows:].astype(jnp.float32)
    out_next = jnp.where(
        solver_side,
        momentum_decay * own_out + grad_out_far.astype(jnp.float32),
        own_out - step_size * (momentum_decay * other_out + grad_out),
    )
    hidden_next = jnp.where(
        solver_side,
        momentum_decay * own_hidden + grad_hidden_far.astype(jnp.float32),
        own_hidden - step_size * (momentum_decay * other_hidden + grad_hidden),
    )
    fields_next = jnp.where(solver_side, advanced, next_batch.astype(jnp.float32))
    return (fields_next[None], out_next[None], hidden_next[None])


def solution(mesh):
    finer = Mesh(
        mesh.devices.reshape(mesh.shape["role"], 2, 4, 4, 2),
        ALL,
    )
    in_specs = (
        P("role", None, TILE),
        P(TILE),
        P(TILE),
        P(),
        P(),
        P("role", None, TILE),
        P("role", None, TILE, None),
    )
    out_specs = (P("role", None, TILE), P("role", None, TILE), P("role", None, TILE, None))
    return jax.shard_map(body, mesh=finer, in_specs=in_specs, out_specs=out_specs, check_vma=False)
```

```python
import itertools

import jax
import jax.numpy as jnp
from jax import lax
from jax.experimental import pallas as pl
from jax.experimental.pallas import tpu as pltpu
from jax.sharding import Mesh
from jax.sharding import PartitionSpec as P

BATCH = 512
LAYERS = 5
TILE = ("tile_0", "tile_1", "tile_2", "tile_3")
PLANE = ("tile_1", "tile_2", "tile_3")
FLOOR = ("tile_1", "tile_2")
CHIPS = ("tile_0", "tile_1", "tile_2")
ALL = ("role", *TILE)

momentum_decay = 0.9
step_size = 0.1


def to_trainer(value):
    return lax.ppermute(value, "role", [(0, 1)])


def to_solver(value):
    return lax.ppermute(value, "role", [(1, 0)])


def swapped(value, axis):
    return lax.ppermute(value, axis, [(0, 1), (1, 0)])


def from_everyone(value, axes):
    copies = jnp.broadcast_to(value, (lax.axis_size(axes), *value.shape))
    return lax.all_to_all(copies, axes, split_axis=0, concat_axis=0, tiled=True)


def ordered(mine, other, place, axis):
    return jnp.where(
        place == 0, jnp.stack([mine, other], axis), jnp.stack([other, mine], axis)
    )


def advance(fields, before, after, velocity, growth):
    states = jnp.concatenate([before[:BATCH, -1:], fields, after[:, :1]], axis=1)
    speeds = jnp.concatenate([before[BATCH, -1:], velocity])
    outflow = (
        jnp.maximum(speeds, 0.0) * states[:, :-1] + jnp.minimum(speeds, 0.0) * states[:, 1:]
    )
    carried = fields - outflow[:, 1:] + outflow[:, :-1]
    return carried + growth * carried * (1.0 - carried)


def from_trainers(value, role):
    pairs = []
    for plane, *place in itertools.product(*map(range, SIZES[1:])):
        pairs.append((flat(SIZES, (1, plane, *place)), flat(SIZES, (role, 1 - plane, *place))))
    return lax.ppermute(value, ALL, pairs)


def flat(sizes, place):
    index = 0
    for size, coordinate in zip(sizes, place):
        index = index * size + coordinate
    return index


def tied(value, *others):
    return lax.optimization_barrier((value, *others))[0]


SIZES = (2, 2, 4, 4, 2)
UNITS = 16
COLUMNS = 256
LANES = 128
VMEM_BYTES = 24 * 1024 * 1024
WIDE_VMEM = 60 * 1024 * 1024


def forward_kernel(
    gathered, features_ref, tiles_ref, last_ref, slopes_out, weights_out,
    weights, inputs, slopes, first_sem, rest_sem, out_sems,
):
    chip = lax.axis_index(CHIPS)
    own_tile = pl.ds(pl.multiple_of((chip * 2 * UNITS // LANES) * LANES, LANES), LANES)
    places = gathered.shape[0]
    plane = lax.axis_index("tile_0")

    def start(first, layers, sem):
        def step(place, carry):
            for number, half in enumerate((plane, 1 - plane)):
                row = pl.multiple_of((half * places + place) * UNITS, UNITS)
                pltpu.make_async_copy(
                    gathered.at[place, number, pl.ds(first, layers)],
                    weights.at[pl.ds(first, layers), pl.ds(row, UNITS)],
                    sem,
                ).start()
            return carry

        lax.fori_loop(0, places, step, 0)

    def finish(first, layers, sem):
        part = weights.at[pl.ds(first, layers)]
        pltpu.make_async_copy(part, part, sem).wait()

    start(0, 1, first_sem)
    start(1, LAYERS - 1, rest_sem)
    inputs[0] = features_ref[...]
    finish(0, 1, first_sem)
    kept = []
    for layer in range(LAYERS):
        if layer == 1:
            finish(1, LAYERS - 1, rest_sem)
            kept.append(
                pltpu.make_async_copy(weights.at[pl.ds(1, LAYERS - 1)], weights_out, out_sems.at[LAYERS])
            )
            kept[-1].start()
        for first in range(0, weights.shape[2], COLUMNS):
            columns = pl.ds(first, COLUMNS)
            total = jnp.dot(
                inputs[layer], weights[layer, :, columns], preferred_element_type=jnp.float32
            )
            logistic = 0.5 + 0.5 * jnp.tanh(0.5 * total)
            activation = total * logistic
            if layer + 1 < LAYERS:
                inputs[layer + 1, :, columns] = activation.astype(jnp.bfloat16)
            else:
                last_ref[:, columns] = activation.astype(jnp.bfloat16)
            slopes[layer, :, columns] = logistic + activation * (1.0 - logistic)
        kept.append(pltpu.make_async_copy(slopes.at[layer], slopes_out.at[layer], out_sems.at[layer]))
        kept[-1].start()
        tiles_ref[layer] = inputs[layer, :, own_tile]
    for copy in kept:
        copy.wait()


def forward(gathered, features):
    rows, width = features.shape
    vmem = pl.BlockSpec(memory_space=pltpu.VMEM)
    hbm = pl.BlockSpec(memory_space=pltpu.HBM)
    return pl.pallas_call(
        forward_kernel,
        out_shape=(
            jax.ShapeDtypeStruct((LAYERS, rows, LANES), jnp.bfloat16),
            jax.ShapeDtypeStruct((rows, width), jnp.bfloat16),
            jax.ShapeDtypeStruct((LAYERS, rows, width), jnp.float32),
            jax.ShapeDtypeStruct((LAYERS - 1, width, width), jnp.bfloat16),
        ),
        in_specs=[hbm, vmem],
        out_specs=(vmem, vmem, hbm, hbm),
        scratch_shapes=[
            pltpu.VMEM((LAYERS, width, width), jnp.bfloat16),
            pltpu.VMEM((LAYERS, rows, width), jnp.bfloat16),
            pltpu.VMEM((LAYERS, rows, width), jnp.float32),
            pltpu.SemaphoreType.DMA(()),
            pltpu.SemaphoreType.DMA(()),
            pltpu.SemaphoreType.DMA((LAYERS + 1,)),
        ],
        compiler_params=pltpu.CompilerParams(vmem_limit_bytes=WIDE_VMEM),
        cost_estimate=pl.CostEstimate(
            flops=2 * LAYERS * rows * width * width,
            bytes_accessed=LAYERS * width * (4 * width + 6 * rows),
            transcendentals=LAYERS * rows * width,
        ),
    )(gathered, features)


def backward_kernel(
    slope_ref, own_inputs_ref, slopes_in, weights, kept_ref, given_ref, kept_narrow, given_narrow,
    held, slopes, slots, sems,
):
    copies = {}
    for layer in range(LAYERS - 1, 0, -1):
        below = layer - 1
        copies[layer] = (
            pltpu.make_async_copy(weights.at[below], held.at[below], sems.at[0, below]),
            pltpu.make_async_copy(slopes_in.at[below], slopes.at[below], sems.at[1, below]),
        )
    for layer in (LAYERS - 1, LAYERS - 2):
        for copy in copies[layer]:
            copy.start()
    now = slope_ref
    for layer in range(LAYERS - 1, -1, -1):
        if layer > 0:
            later = slots.at[layer % 2]
            for copy in copies[layer]:
                copy.wait()
            for copy in copies.get(layer - 2, ()):
                copy.start()
            for first in range(0, held.shape[1], COLUMNS):
                columns = pl.ds(first, COLUMNS)
                upstream = lax.dot_general(
                    now[...],
                    held[layer - 1, columns, :],
                    (((1,), (1,)), ((), ())),
                    preferred_element_type=jnp.float32,
                )
                later[:, columns] = (upstream * slopes[layer - 1, :, columns]).astype(jnp.bfloat16)
        grads = jnp.dot(own_inputs_ref[layer], now[...], preferred_element_type=jnp.float32)
        kept_ref[layer] = grads[:UNITS]
        given_ref[layer] = grads[UNITS:]
        kept_narrow[layer] = grads[:UNITS].astype(jnp.bfloat16)
        given_narrow[layer] = grads[UNITS:].astype(jnp.bfloat16)
        if layer > 0:
            now = later


def backward(slope, own_inputs, slopes, weights):
    rows, width = slope.shape
    vmem = pl.BlockSpec(memory_space=pltpu.VMEM)
    hbm = pl.BlockSpec(memory_space=pltpu.HBM)
    return pl.pallas_call(
        backward_kernel,
        out_shape=tuple(
            jax.ShapeDtypeStruct((LAYERS, UNITS, width), kind)
            for kind in (jnp.float32, jnp.float32, jnp.bfloat16, jnp.bfloat16)
        ),
        in_specs=[vmem, vmem, hbm, hbm],
        out_specs=(vmem,) * 4,
        scratch_shapes=[
            pltpu.VMEM((LAYERS - 1, width, width), jnp.bfloat16),
            pltpu.VMEM((LAYERS - 1, rows, width), jnp.float32),
            pltpu.VMEM((2, rows, width), jnp.bfloat16),
            pltpu.SemaphoreType.DMA((2, LAYERS - 1)),
        ],
        compiler_params=pltpu.CompilerParams(vmem_limit_bytes=WIDE_VMEM),
        cost_estimate=pl.CostEstimate(
            flops=2 * (LAYERS - 1) * rows * width * width,
            bytes_accessed=LAYERS * width * (2 * width + 4 * rows),
            transcendentals=0,
        ),
    )(slope, own_inputs, slopes, weights)


def output_kernel(place_ref, activation_ref, fields_ref, weights_ref, left_ref, right_ref, partial_ref, residual_ref):
    del place_ref
    chunk = left_ref.shape[1]
    for first in range(0, weights_ref.shape[1], COLUMNS):
        columns = pl.ds(first, COLUMNS)
        predicted = jnp.dot(
            activation_ref[...], weights_ref[:, columns], preferred_element_type=jnp.float32
        )
        residual = ((predicted - fields_ref[:, columns]) / BATCH).astype(jnp.bfloat16)
        residual_ref[:, columns] = residual
        part = left_ref if first < chunk else right_ref
        part[:, first % chunk : first % chunk + COLUMNS] = residual
    for first in range(0, weights_ref.shape[0], COLUMNS):
        columns = pl.ds(first, COLUMNS)
        partial_ref[:, columns] = lax.dot_general(
            residual_ref[...],
            weights_ref[columns, :],
            (((1,), (1,)), ((), ())),
            preferred_element_type=jnp.float32,
        ).astype(partial_ref.dtype)


def output_layer(place, activation, fields, weights, kind):
    rows, width = activation.shape
    cells = fields.shape[1]
    return pl.pallas_call(
        output_kernel,
        out_shape=(
            jax.ShapeDtypeStruct((rows, cells // 2), jnp.bfloat16),
            jax.ShapeDtypeStruct((rows, cells // 2), jnp.bfloat16),
            jax.ShapeDtypeStruct((rows, width), kind),
        ),
        grid_spec=pltpu.PrefetchScalarGridSpec(
            num_scalar_prefetch=1,
            grid=(1,),
            in_specs=[
                pl.BlockSpec((rows, width), lambda i, place: (0, 0)),
                pl.BlockSpec((rows, cells), lambda i, place: (place[0], 0)),
                pl.BlockSpec((width, cells), lambda i, place: (0, 0)),
            ],
            out_specs=(
                pl.BlockSpec((rows, cells // 2), lambda i, place: (0, 0)),
                pl.BlockSpec((rows, cells // 2), lambda i, place: (0, 0)),
                pl.BlockSpec((rows, width), lambda i, place: (0, 0)),
            ),
            scratch_shapes=[pltpu.VMEM((rows, cells), jnp.bfloat16)],
        ),
        compiler_params=pltpu.CompilerParams(vmem_limit_bytes=VMEM_BYTES),
        cost_estimate=pl.CostEstimate(
            flops=4 * rows * width * cells,
            bytes_accessed=2 * width * cells + 12 * rows * cells,
            transcendentals=0,
        ),
    )(place, activation, fields, weights)


def update_kernel(
    solver_ref, own_ref, other_ref, last_ref, other_last_ref, here_ref, far_ref, begun, next_ref, residual
):
    del begun
    solver_side = solver_ref[0] == 1
    half = last_ref.shape[0]

    @pl.when(jnp.logical_and(pl.program_id(0) == 0, solver_side))
    def _():
        residual[...] = far_ref[...]

    @pl.when(jnp.logical_and(pl.program_id(0) == 0, jnp.logical_not(solver_side)))
    def _():
        residual[...] = here_ref[...]

    gradient = lax.dot_general(
        last_ref[...], residual[:half], (((0,), (0,)), ((), ())), preferred_element_type=jnp.float32
    ) + lax.dot_general(
        other_last_ref[...], residual[half:], (((0,), (0,)), ((), ())), preferred_element_type=jnp.float32
    )

    @pl.when(solver_side)
    def _():
        next_ref[...] = momentum_decay * own_ref[...] + gradient

    @pl.when(jnp.logical_not(solver_side))
    def _():
        momentum = momentum_decay * other_ref[...].astype(jnp.float32) + gradient
        next_ref[...] = own_ref[...] - step_size * momentum


def updated(chunk, begun, solver_side, own, other, last, other_last, here, far):
    width, cells = own.shape
    half = last.shape[0]
    columns = pl.BlockSpec((half, BLOCK), lambda i, flag: (0, i))
    whole = pl.BlockSpec((2 * half, cells // 2), lambda i, flag: (0, 0))
    block = pl.BlockSpec((BLOCK, cells // 2), lambda i, flag: (i, chunk))
    return pl.pallas_call(
        update_kernel,
        out_shape=jax.ShapeDtypeStruct(own.shape, jnp.float32),
        grid_spec=pltpu.PrefetchScalarGridSpec(
            num_scalar_prefetch=1,
            grid=(width // BLOCK,),
            in_specs=[
                block,
                pl.BlockSpec((BLOCK, cells // 2), lambda i, flag: (i, 0)),
                columns,
                columns,
                whole,
                whole,
                pl.BlockSpec(memory_space=pl.ANY),
            ],
            out_specs=block,
            scratch_shapes=[pltpu.VMEM((2 * half, cells // 2), jnp.bfloat16)],
        ),
        input_output_aliases={} if begun is None else {7: 0},
        compiler_params=pltpu.CompilerParams(vmem_limit_bytes=VMEM_BYTES),
        cost_estimate=pl.CostEstimate(
            flops=2 * half * width * cells, bytes_accessed=5 * width * cells, transcendentals=0
        ),
    )(
        solver_side.astype(jnp.int32)[None], own, other, last, other_last, here, far,
        jnp.zeros((8, LANES), jnp.float32) if begun is None else begun,
    )


BLOCK = 256


def body(fields_pair, velocity, growth, features, assignment, out_pair, hidden_pair):
    solver_side = lax.axis_index("role") == 0
    core = lax.axis_index("tile_3")
    chip = lax.axis_index(CHIPS)
    fields = fields_pair[0]
    own_out = out_pair[0]
    own_hidden = hidden_pair[0]
    units = own_hidden.shape[1]
    width = own_hidden.shape[2]
    half = BATCH // 2

    hidden_narrow = own_hidden.astype(jnp.bfloat16)
    out_narrow = own_out.astype(jnp.bfloat16)
    edge = jnp.concatenate(
        [fields[:, -128:], jnp.broadcast_to(velocity[None, -128:], (8, 128))], axis=0
    )

    partner_hidden = swapped(hidden_narrow, "role")
    near = jnp.where(solver_side, partner_hidden, hidden_narrow)
    far = jnp.where(solver_side, from_trainers(hidden_narrow, 0), from_trainers(hidden_narrow, 1))
    gathered = lax.all_gather(jnp.stack([near, far]), PLANE, axis=0)

    middle = own_out.shape[1] // 2
    momentum = to_trainer(own_out[:, :middle].astype(jnp.bfloat16))
    count = lax.axis_size(TILE)
    up = [(i, (i + 1) % count) for i in range(count)]
    down = [(j, i) for i, j in up]
    before = lax.ppermute(edge, TILE, up)
    after = lax.ppermute(fields[:, :128], TILE, down)
    advanced = advance(fields, before, after, velocity, growth)
    carried = jnp.take(advanced.astype(jnp.bfloat16), assignment, axis=0)
    next_batch = to_trainer(carried)
    gathered, advanced, momentum, next_batch = lax.optimization_barrier(
        (gathered, advanced, momentum, next_batch)
    )
    tiles, last, slopes, weights = forward(
        gathered, lax.dynamic_slice_in_dim(features, core * half, half, 0)
    )
    place = core.astype(jnp.int32)[None]
    other_last = swapped(last, "tile_3")
    left, right, kept = output_layer(place, last, fields, out_narrow, jnp.float32)
    other_left, other_right, given = output_layer(
        1 - place, tied(other_last, kept), fields, out_narrow, jnp.bfloat16
    )
    arrived = swapped(given, "tile_3")
    chip_sum = (kept + arrived.astype(jnp.float32)).astype(jnp.bfloat16)
    chips = lax.axis_size(FLOOR)
    rows = half // chips
    first = lax.axis_index(FLOOR) * rows
    shares = lax.all_to_all(
        chip_sum.reshape(chips, rows, width), FLOOR, split_axis=0, concat_axis=0, tiled=True
    )
    plane_sum = shares.astype(jnp.float32).sum(axis=0)
    upstream = plane_sum + swapped(plane_sum, "tile_0")
    upstream, left, right, rest = lax.optimization_barrier(
        (
            upstream,
            jnp.concatenate([left, other_left]),
            jnp.concatenate([right, other_right]),
            own_out[:, middle:].astype(jnp.bfloat16),
        )
    )
    left_far, right_far, momentum_rest = to_solver(left), to_solver(right), to_trainer(rest)
    own_factor = lax.dynamic_slice_in_dim(slopes[LAYERS - 1], first, rows, 0)
    own_slope = (upstream * own_factor).astype(jnp.bfloat16)
    slope = from_everyone(own_slope, FLOOR).reshape(half, width)

    own_inputs = jnp.concatenate(
        [
            lax.dynamic_slice_in_dim(tiles, (chip * 2 + side) * units % LANES, units, 2)
            for side in (core, 1 - core)
        ],
        axis=2,
    )
    slope, own_inputs = lax.optimization_barrier((slope, own_inputs.swapaxes(1, 2)))
    kept, given, kept_narrow, given_narrow = backward(slope, own_inputs, slopes, weights)
    crossing = [
        (flat(SIZES, (1, *place, core)), flat(SIZES, (0, *place, 1 - core)))
        for *place, core in itertools.product(*map(range, SIZES[1:]))
    ]
    kept_far = to_solver(kept_narrow)
    given_far = lax.ppermute(given_narrow, ALL, crossing)
    grad_hidden = kept + swapped(given, "tile_3")
    grad_hidden_far = kept_far.astype(jnp.float32) + given_far.astype(jnp.float32)

    other_hidden = partner_hidden.astype(jnp.float32)
    out_next = updated(
        0, None, solver_side, own_out, momentum, last, other_last, left, left_far
    )
    out_next = updated(
        1, out_next, solver_side, own_out, momentum_rest, last, other_last, right, right_far
    )
    hidden_next = jnp.where(
        solver_side,
        momentum_decay * own_hidden + grad_hidden_far,
        own_hidden - step_size * (momentum_decay * other_hidden + grad_hidden),
    )
    fields_next = jnp.where(solver_side, advanced, next_batch.astype(jnp.float32))
    return (fields_next[None], out_next[None], hidden_next[None])


def solution(mesh):
    finer = Mesh(
        mesh.devices.reshape(SIZES), ALL
    )
    in_specs = (
        P("role", None, TILE),
        P(TILE),
        P(TILE),
        P(),
        P(),
        P("role", None, TILE),
        P("role", None, TILE, None),
    )
    out_specs = (P("role", None, TILE), P("role", None, TILE), P("role", None, TILE, None))
    return jax.shard_map(body, mesh=finer, in_specs=in_specs, out_specs=out_specs, check_vma=False)
```

```python
import itertools

import jax
import jax.numpy as jnp
from jax import lax
from jax.experimental import pallas as pl
from jax.experimental.pallas import tpu as pltpu
from jax.sharding import Mesh
from jax.sharding import PartitionSpec as P

BATCH = 512
LAYERS = 5
TILE = ("tile_0", "tile_1", "tile_2", "tile_3")
PLANE = ("tile_1", "tile_2", "tile_3")
FLOOR = ("tile_1", "tile_2")
CHIPS = ("tile_0", "tile_1", "tile_2")
ALL = ("role", *TILE)

momentum_decay = 0.9
step_size = 0.1


def to_trainer(value):
    return lax.ppermute(value, "role", [(0, 1)])


def to_solver(value):
    return lax.ppermute(value, "role", [(1, 0)])


def swapped(value, axis):
    return lax.ppermute(value, axis, [(0, 1), (1, 0)])


def from_everyone(value, axes):
    copies = jnp.broadcast_to(value, (lax.axis_size(axes), *value.shape))
    return lax.all_to_all(copies, axes, split_axis=0, concat_axis=0, tiled=True)


def ordered(mine, other, place, axis):
    return jnp.where(
        place == 0, jnp.stack([mine, other], axis), jnp.stack([other, mine], axis)
    )


def advance(fields, before, after, velocity, growth):
    states = jnp.concatenate([before[:BATCH, -1:], fields, after[:, :1]], axis=1)
    speeds = jnp.concatenate([before[BATCH, -1:], velocity])
    outflow = (
        jnp.maximum(speeds, 0.0) * states[:, :-1] + jnp.minimum(speeds, 0.0) * states[:, 1:]
    )
    carried = fields - outflow[:, 1:] + outflow[:, :-1]
    return carried + growth * carried * (1.0 - carried)


def from_trainers(value, role):
    pairs = []
    for plane, *place in itertools.product(*map(range, SIZES[1:])):
        pairs.append((flat(SIZES, (1, plane, *place)), flat(SIZES, (role, 1 - plane, *place))))
    return lax.ppermute(value, ALL, pairs)


def flat(sizes, place):
    index = 0
    for size, coordinate in zip(sizes, place):
        index = index * size + coordinate
    return index


def tied(value, *others):
    return lax.optimization_barrier((value, *others))[0]


SIZES = (2, 2, 4, 4, 2)
UNITS = 16
AHEAD = 3
CUT = 512
COLUMNS = 256
LANES = 128
VMEM_BYTES = 24 * 1024 * 1024
WIDE_VMEM = 60 * 1024 * 1024
FORWARD_VMEM = 57 * 1024 * 1024


def fetch(gathered, layer, weights, sem):
    plane = lax.axis_index("tile_0")
    places = gathered.shape[0]

    def step(place, carry):
        for number, half in enumerate((plane, 1 - plane)):
            row = pl.multiple_of((half * places + place) * UNITS, UNITS)
            pltpu.make_async_copy(
                gathered.at[place, number, layer], weights.at[layer, pl.ds(row, UNITS)], sem
            ).start()
        return carry

    lax.fori_loop(0, places, step, 0)


def forward_kernel(
    gathered, features_ref, tiles_ref, last_ref, slopes_out, weights_out,
    weights, inputs, slopes, in_sems, out_sems,
):
    chip = lax.axis_index(CHIPS)
    own_tile = pl.ds(pl.multiple_of((chip * 2 * UNITS // LANES) * LANES, LANES), LANES)
    for layer in range(AHEAD):
        fetch(gathered, layer, weights, in_sems.at[layer])
    inputs[0] = features_ref[...]
    kept = []
    for layer in range(LAYERS):
        part = weights.at[layer]
        pltpu.make_async_copy(part, part, in_sems.at[layer]).wait()
        if layer + AHEAD < LAYERS:
            fetch(gathered, layer + AHEAD, weights, in_sems.at[layer + AHEAD])
        if layer > 0:
            kept.append(
                pltpu.make_async_copy(part, weights_out.at[layer - 1], out_sems.at[LAYERS - 1 + layer])
            )
            kept[-1].start()
        for first in range(0, weights.shape[2], COLUMNS):
            columns = pl.ds(first, COLUMNS)
            total = jnp.dot(
                inputs[layer], weights[layer, :, columns], preferred_element_type=jnp.float32
            )
            logistic = 0.5 + 0.5 * jnp.tanh(0.5 * total)
            activation = total * logistic
            if layer + 1 < LAYERS:
                inputs[layer + 1, :, columns] = activation.astype(jnp.bfloat16)
            else:
                last_ref[:, columns] = activation.astype(jnp.bfloat16)
            slopes[layer, :, columns] = logistic + activation * (1.0 - logistic)
        kept.append(pltpu.make_async_copy(slopes.at[layer], slopes_out.at[layer], out_sems.at[layer]))
        kept[-1].start()
        tiles_ref[layer] = inputs[layer, :, own_tile]
    for copy in kept:
        copy.wait()


def forward(gathered, features):
    rows, width = features.shape
    vmem = pl.BlockSpec(memory_space=pltpu.VMEM)
    hbm = pl.BlockSpec(memory_space=pltpu.HBM)
    return pl.pallas_call(
        forward_kernel,
        out_shape=(
            jax.ShapeDtypeStruct((LAYERS, rows, LANES), jnp.bfloat16),
            jax.ShapeDtypeStruct((rows, width), jnp.bfloat16),
            jax.ShapeDtypeStruct((LAYERS, rows, width), jnp.float32),
            jax.ShapeDtypeStruct((LAYERS - 1, width, width), jnp.bfloat16),
        ),
        in_specs=[hbm, vmem],
        out_specs=(vmem, vmem, hbm, hbm),
        scratch_shapes=[
            pltpu.VMEM((LAYERS, width, width), jnp.bfloat16),
            pltpu.VMEM((LAYERS, rows, width), jnp.bfloat16),
            pltpu.VMEM((LAYERS, rows, width), jnp.float32),
            pltpu.SemaphoreType.DMA((LAYERS,)),
            pltpu.SemaphoreType.DMA((2 * LAYERS - 1,)),
        ],
        compiler_params=pltpu.CompilerParams(vmem_limit_bytes=FORWARD_VMEM),
        cost_estimate=pl.CostEstimate(
            flops=2 * LAYERS * rows * width * width,
            bytes_accessed=LAYERS * width * (4 * width + 6 * rows),
            transcendentals=LAYERS * rows * width,
        ),
    )(gathered, features)


def backward_kernel(
    slope_ref, own_inputs_ref, slopes_in, weights, kept_ref, given_ref, kept_narrow, given_narrow,
    held, slopes, slots, sems,
):
    copies = {}
    for layer in range(LAYERS - 1, 0, -1):
        below = layer - 1
        copies[layer] = (
            pltpu.make_async_copy(weights.at[below], held.at[below], sems.at[0, below]),
            pltpu.make_async_copy(slopes_in.at[below], slopes.at[below], sems.at[1, below]),
        )
    for layer in (LAYERS - 1, LAYERS - 2):
        for copy in copies[layer]:
            copy.start()
    now = slope_ref
    for layer in range(LAYERS - 1, -1, -1):
        if layer > 0:
            later = slots.at[layer % 2]
            for copy in copies[layer]:
                copy.wait()
            for copy in copies.get(layer - 2, ()):
                copy.start()
            for first in range(0, held.shape[1], COLUMNS):
                columns = pl.ds(first, COLUMNS)
                upstream = lax.dot_general(
                    now[...],
                    held[layer - 1, columns, :],
                    (((1,), (1,)), ((), ())),
                    preferred_element_type=jnp.float32,
                )
                later[:, columns] = (upstream * slopes[layer - 1, :, columns]).astype(jnp.bfloat16)
        grads = jnp.dot(own_inputs_ref[layer], now[...], preferred_element_type=jnp.float32)
        kept_ref[layer] = grads[:UNITS]
        given_ref[layer] = grads[UNITS:]
        kept_narrow[layer] = grads[:UNITS].astype(jnp.bfloat16)
        given_narrow[layer] = grads[UNITS:].astype(jnp.bfloat16)
        if layer > 0:
            now = later


def backward(slope, own_inputs, slopes, weights):
    rows, width = slope.shape
    vmem = pl.BlockSpec(memory_space=pltpu.VMEM)
    hbm = pl.BlockSpec(memory_space=pltpu.HBM)
    return pl.pallas_call(
        backward_kernel,
        out_shape=tuple(
            jax.ShapeDtypeStruct((LAYERS, UNITS, width), kind)
            for kind in (jnp.float32, jnp.float32, jnp.bfloat16, jnp.bfloat16)
        ),
        in_specs=[vmem, vmem, hbm, hbm],
        out_specs=(vmem,) * 4,
        scratch_shapes=[
            pltpu.VMEM((LAYERS - 1, width, width), jnp.bfloat16),
            pltpu.VMEM((LAYERS - 1, rows, width), jnp.float32),
            pltpu.VMEM((2, rows, width), jnp.bfloat16),
            pltpu.SemaphoreType.DMA((2, LAYERS - 1)),
        ],
        compiler_params=pltpu.CompilerParams(vmem_limit_bytes=WIDE_VMEM),
        cost_estimate=pl.CostEstimate(
            flops=2 * (LAYERS - 1) * rows * width * width,
            bytes_accessed=LAYERS * width * (2 * width + 4 * rows),
            transcendentals=0,
        ),
    )(slope, own_inputs, slopes, weights)


def output_kernel(place_ref, activation_ref, fields_ref, weights_ref, left_ref, right_ref, partial_ref, residual_ref):
    del place_ref
    for first in range(0, weights_ref.shape[1], COLUMNS):
        columns = pl.ds(first, COLUMNS)
        predicted = jnp.dot(
            activation_ref[...], weights_ref[:, columns], preferred_element_type=jnp.float32
        )
        residual = ((predicted - fields_ref[:, columns]) / BATCH).astype(jnp.bfloat16)
        residual_ref[:, columns] = residual
        if first < CUT:
            left_ref[:, columns] = residual
        else:
            right_ref[:, first - CUT : first - CUT + COLUMNS] = residual
    for first in range(0, weights_ref.shape[0], COLUMNS):
        columns = pl.ds(first, COLUMNS)
        partial_ref[:, columns] = lax.dot_general(
            residual_ref[...],
            weights_ref[columns, :],
            (((1,), (1,)), ((), ())),
            preferred_element_type=jnp.float32,
        ).astype(partial_ref.dtype)


def output_layer(place, activation, fields, weights, kind):
    rows, width = activation.shape
    cells = fields.shape[1]
    return pl.pallas_call(
        output_kernel,
        out_shape=(
            jax.ShapeDtypeStruct((rows, CUT), jnp.bfloat16),
            jax.ShapeDtypeStruct((rows, cells - CUT), jnp.bfloat16),
            jax.ShapeDtypeStruct((rows, width), kind),
        ),
        grid_spec=pltpu.PrefetchScalarGridSpec(
            num_scalar_prefetch=1,
            grid=(1,),
            in_specs=[
                pl.BlockSpec((rows, width), lambda i, place: (0, 0)),
                pl.BlockSpec((rows, cells), lambda i, place: (place[0], 0)),
                pl.BlockSpec((width, cells), lambda i, place: (0, 0)),
            ],
            out_specs=(
                pl.BlockSpec((rows, CUT), lambda i, place: (0, 0)),
                pl.BlockSpec((rows, cells - CUT), lambda i, place: (0, 0)),
                pl.BlockSpec((rows, width), lambda i, place: (0, 0)),
            ),
            scratch_shapes=[pltpu.VMEM((rows, cells), jnp.bfloat16)],
        ),
        compiler_params=pltpu.CompilerParams(vmem_limit_bytes=VMEM_BYTES),
        cost_estimate=pl.CostEstimate(
            flops=4 * rows * width * cells,
            bytes_accessed=2 * width * cells + 12 * rows * cells,
            transcendentals=0,
        ),
    )(place, activation, fields, weights)


def update_kernel(
    solver_ref, own_ref, upper_ref, lower_ref, last_ref, other_last_ref, here_ref, far_ref, begun, next_ref, residual
):
    del begun
    solver_side = solver_ref[0] == 1
    step = pl.program_id(0)
    upper = step < pl.num_programs(0) // 2
    half = last_ref.shape[0]

    @pl.when(jnp.logical_and(step == 0, solver_side))
    def _():
        residual[...] = far_ref[...]

    @pl.when(jnp.logical_and(step == 0, jnp.logical_not(solver_side)))
    def _():
        residual[...] = here_ref[...]

    gradient = lax.dot_general(
        last_ref[...], residual[:half], (((0,), (0,)), ((), ())), preferred_element_type=jnp.float32
    ) + lax.dot_general(
        other_last_ref[...], residual[half:], (((0,), (0,)), ((), ())), preferred_element_type=jnp.float32
    )

    def trained(other_ref):
        momentum = momentum_decay * other_ref[...].astype(jnp.float32) + gradient
        next_ref[...] = own_ref[...] - step_size * momentum

    @pl.when(solver_side)
    def _():
        next_ref[...] = momentum_decay * own_ref[...] + gradient

    @pl.when(jnp.logical_and(upper, jnp.logical_not(solver_side)))
    def _():
        trained(upper_ref)

    @pl.when(jnp.logical_not(jnp.logical_or(upper, solver_side)))
    def _():
        trained(lower_ref)


def updated(begun, solver_side, own, upper, lower, last, other_last, here, far):
    width, cells = own.shape
    size = here.shape[1]
    steps = width // BLOCK
    chunk = 0 if begun is None else 1
    skipped = 0 if lower.shape[0] == width else steps // 2
    half = last.shape[0]
    columns = pl.BlockSpec((half, BLOCK), lambda i, flag: (0, i))
    whole = pl.BlockSpec((2 * half, size), lambda i, flag: (0, 0))
    block = pl.BlockSpec((BLOCK, size), lambda i, flag: (i, chunk))
    return pl.pallas_call(
        update_kernel,
        out_shape=jax.ShapeDtypeStruct(own.shape, jnp.float32),
        grid_spec=pltpu.PrefetchScalarGridSpec(
            num_scalar_prefetch=1,
            grid=(steps,),
            in_specs=[
                block,
                pl.BlockSpec((BLOCK, size), lambda i, flag: (jnp.minimum(i, steps // 2 - 1), 0)),
                pl.BlockSpec((BLOCK, size), lambda i, flag: (jnp.maximum(i, steps // 2) - skipped, 0)),
                columns,
                columns,
                whole,
                whole,
                pl.BlockSpec(memory_space=pl.ANY),
            ],
            out_specs=block,
            scratch_shapes=[pltpu.VMEM((2 * half, size), jnp.bfloat16)],
        ),
        input_output_aliases={} if begun is None else {8: 0},
        compiler_params=pltpu.CompilerParams(
            vmem_limit_bytes=WIDE_VMEM if begun is None else VMEM_BYTES
        ),
        cost_estimate=pl.CostEstimate(
            flops=4 * half * width * size, bytes_accessed=10 * width * size, transcendentals=0
        ),
    )(
        solver_side.astype(jnp.int32)[None], own, upper, lower, last, other_last, here, far,
        own if begun is None else begun,
    )


BLOCK = 256


def body(fields_pair, velocity, growth, features, assignment, out_pair, hidden_pair):
    solver_side = lax.axis_index("role") == 0
    core = lax.axis_index("tile_3")
    chip = lax.axis_index(CHIPS)
    fields = fields_pair[0]
    own_out = out_pair[0]
    own_hidden = hidden_pair[0]
    units = own_hidden.shape[1]
    width = own_hidden.shape[2]
    half = BATCH // 2

    hidden_narrow = own_hidden.astype(jnp.bfloat16)
    first_narrow = own_out[:, :CUT].astype(jnp.bfloat16)
    upper_narrow = own_out[:BATCH, CUT:].astype(jnp.bfloat16)
    lower_narrow = own_out[BATCH:, CUT:].astype(jnp.bfloat16)
    partner_hidden = swapped(hidden_narrow, "role")
    near = jnp.where(solver_side, partner_hidden, hidden_narrow)
    far = jnp.where(solver_side, from_trainers(hidden_narrow, 0), from_trainers(hidden_narrow, 1))
    gathered = lax.all_gather(jnp.stack([near, far]), PLANE, axis=0)

    momentum = to_trainer(first_narrow)
    early, first_narrow = lax.optimization_barrier((fields, first_narrow))
    edge = jnp.concatenate(
        [early[:, -128:], jnp.broadcast_to(velocity[None, -128:], (8, 128))], axis=0
    )

    count = lax.axis_size(TILE)
    up = [(i, (i + 1) % count) for i in range(count)]
    down = [(j, i) for i, j in up]
    before = lax.ppermute(edge, TILE, up)
    after = lax.ppermute(early[:, :128], TILE, down)
    out_narrow = tied(own_out, before, after).astype(jnp.bfloat16)
    advanced = advance(fields, before, after, velocity, growth)
    carried = jnp.take(advanced.astype(jnp.bfloat16), assignment, axis=0)
    next_batch = to_trainer(carried)
    gathered, advanced, momentum, next_batch, out_narrow = lax.optimization_barrier(
        (gathered, advanced, momentum, next_batch, out_narrow)
    )
    fields_next = jnp.where(solver_side, advanced, next_batch.astype(jnp.float32))
    tiles, last, slopes, weights = forward(
        gathered, lax.dynamic_slice_in_dim(features, core * half, half, 0)
    )
    place = core.astype(jnp.int32)[None]
    other_last = swapped(last, "tile_3")
    left, right, kept = output_layer(place, last, fields, out_narrow, jnp.float32)
    other_left, other_right, given = output_layer(
        1 - place, tied(other_last, kept), fields, out_narrow, jnp.bfloat16
    )
    arrived = swapped(given, "tile_3")
    chip_sum = (kept + arrived.astype(jnp.float32)).astype(jnp.bfloat16)
    chips = lax.axis_size(FLOOR)
    rows = half // chips
    first = lax.axis_index(FLOOR) * rows
    shares = lax.all_to_all(
        chip_sum.reshape(chips, rows, width), FLOOR, split_axis=0, concat_axis=0, tiled=True
    )
    left = jnp.concatenate([left, other_left])
    left_far = swapped(jnp.where(solver_side, upper_narrow, left), "role")
    right = jnp.concatenate([right, other_right])
    payload = jnp.where(solver_side, lower_narrow, right)
    shares, left_far, fields_next, payload = lax.optimization_barrier(
        (shares, left_far, fields_next, payload)
    )
    plane_sum = shares.astype(jnp.float32).sum(axis=0)
    upstream = plane_sum + swapped(plane_sum, "tile_0")
    own_factor = lax.dynamic_slice_in_dim(slopes[LAYERS - 1], first, rows, 0)
    own_slope = (upstream * own_factor).astype(jnp.bfloat16)
    slope = from_everyone(own_slope, FLOOR).reshape(half, width)

    tiles = tied(tiles, own_slope)
    own_inputs = jnp.concatenate(
        [
            lax.dynamic_slice_in_dim(tiles, (chip * 2 + side) * units % LANES, units, 2)
            for side in (core, 1 - core)
        ],
        axis=2,
    ).swapaxes(1, 2)
    right_far = swapped(tied(payload, own_inputs), "role")
    out_next = updated(
        None, solver_side, own_out, momentum, momentum, last, other_last, left, left_far
    )
    slope, own_inputs, out_next = lax.optimization_barrier((slope, own_inputs, out_next))
    kept, given, kept_narrow, given_narrow = backward(slope, own_inputs, slopes, weights)
    kept_narrow, given_narrow, right_far = lax.optimization_barrier(
        (kept_narrow, given_narrow, right_far)
    )
    crossing = [
        (flat(SIZES, (1, *place, core)), flat(SIZES, (0, *place, 1 - core)))
        for *place, core in itertools.product(*map(range, SIZES[1:]))
    ]
    kept_far = to_solver(kept_narrow)
    given_far = lax.ppermute(given_narrow, ALL, crossing)
    grad_hidden = kept + swapped(given, "tile_3")
    grad_hidden_far = kept_far.astype(jnp.float32) + given_far.astype(jnp.float32)

    other_hidden = partner_hidden.astype(jnp.float32)
    out_next = updated(
        out_next, solver_side, own_out, left_far, right_far, last, other_last, right, right_far
    )
    hidden_next = jnp.where(
        solver_side,
        momentum_decay * own_hidden + grad_hidden_far,
        own_hidden - step_size * (momentum_decay * other_hidden + grad_hidden),
    )
    return (fields_next[None], out_next[None], hidden_next[None])


def solution(mesh):
    finer = Mesh(
        mesh.devices.reshape(SIZES), ALL
    )
    in_specs = (
        P("role", None, TILE),
        P(TILE),
        P(TILE),
        P(),
        P(),
        P("role", None, TILE),
        P("role", None, TILE, None),
    )
    out_specs = (P("role", None, TILE), P("role", None, TILE), P("role", None, TILE, None))
    return jax.shard_map(body, mesh=finer, in_specs=in_specs, out_specs=out_specs, check_vma=False)
```

```python
import itertools

import jax
import jax.numpy as jnp
from jax import lax
from jax.experimental import pallas as pl
from jax.experimental.pallas import tpu as pltpu
from jax.sharding import Mesh
from jax.sharding import PartitionSpec as P

BATCH = 512
LAYERS = 5
TILE = ("tile_0", "tile_1", "tile_2", "tile_3")
PLANE = ("tile_1", "tile_2", "tile_3")
FLOOR = ("tile_1", "tile_2")
CHIPS = ("tile_0", "tile_1", "tile_2")
ALL = ("role", *TILE)

momentum_decay = 0.9
step_size = 0.1


def to_trainer(value):
    return lax.ppermute(value, "role", [(0, 1)])


def to_solver(value):
    return lax.ppermute(value, "role", [(1, 0)])


def swapped(value, axis):
    return lax.ppermute(value, axis, [(0, 1), (1, 0)])


def from_everyone(value, axes):
    copies = jnp.broadcast_to(value, (lax.axis_size(axes), *value.shape))
    return lax.all_to_all(copies, axes, split_axis=0, concat_axis=0, tiled=True)


def ordered(mine, other, place, axis):
    return jnp.where(
        place == 0, jnp.stack([mine, other], axis), jnp.stack([other, mine], axis)
    )


def advance(fields, before, after, velocity, growth):
    states = jnp.concatenate([before[:BATCH, -1:], fields, after[:, :1]], axis=1)
    speeds = jnp.concatenate([before[BATCH, -1:], velocity])
    outflow = (
        jnp.maximum(speeds, 0.0) * states[:, :-1] + jnp.minimum(speeds, 0.0) * states[:, 1:]
    )
    carried = fields - outflow[:, 1:] + outflow[:, :-1]
    return carried + growth * carried * (1.0 - carried)


def from_trainers(value, role):
    pairs = []
    for plane, *place in itertools.product(*map(range, SIZES[1:])):
        pairs.append((flat(SIZES, (1, plane, *place)), flat(SIZES, (role, 1 - plane, *place))))
    return lax.ppermute(value, ALL, pairs)


def flat(sizes, place):
    index = 0
    for size, coordinate in zip(sizes, place):
        index = index * size + coordinate
    return index


def tied(value, *others):
    return lax.optimization_barrier((value, *others))[0]


SIZES = (2, 2, 4, 4, 2)
UNITS = 16
AHEAD = 5
CUT = 512
COLUMNS = 256
LANES = 128
VMEM_BYTES = 24 * 1024 * 1024
WIDE_VMEM = 60 * 1024 * 1024
FORWARD_VMEM = 57 * 1024 * 1024


def fetch(gathered, layer, weights, to, sem):
    plane = lax.axis_index("tile_0")
    places = gathered.shape[0]

    def step(place, carry):
        for number, half in enumerate((plane, 1 - plane)):
            row = pl.multiple_of((half * places + place) * UNITS, UNITS)
            pltpu.make_async_copy(
                gathered.at[place, number, layer], weights.at[to, pl.ds(row, UNITS)], sem
            ).start()
        return carry

    lax.fori_loop(0, places, step, 0)


def forward_kernel(
    gathered, features_ref, tiles_ref, last_ref, slopes_out,
    weights, inputs, slopes, in_sems, out_sems,
):
    chip = lax.axis_index(CHIPS)
    own_tile = pl.ds(pl.multiple_of((chip * 2 * UNITS // LANES) * LANES, LANES), LANES)
    for layer in range(AHEAD):
        fetch(gathered, layer, weights, layer, in_sems.at[layer])
    inputs[0] = features_ref[...]
    kept = []
    for layer in range(LAYERS):
        part = weights.at[layer]
        pltpu.make_async_copy(part, part, in_sems.at[layer]).wait()
        if layer + AHEAD < LAYERS:
            later = layer + AHEAD
            fetch(gathered, later, weights, later, in_sems.at[later])
        for first in range(0, weights.shape[2], COLUMNS):
            columns = pl.ds(first, COLUMNS)
            total = jnp.dot(
                inputs[layer], weights[layer, :, columns], preferred_element_type=jnp.float32
            )
            logistic = 0.5 + 0.5 * jnp.tanh(0.5 * total)
            activation = total * logistic
            if layer + 1 < LAYERS:
                inputs[layer + 1, :, columns] = activation.astype(jnp.bfloat16)
            else:
                last_ref[:, columns] = activation.astype(jnp.bfloat16)
            slopes[layer, :, columns] = logistic + activation * (1.0 - logistic)
        kept.append(pltpu.make_async_copy(slopes.at[layer], slopes_out.at[layer], out_sems.at[layer]))
        kept[-1].start()
        tiles_ref[layer] = inputs[layer, :, own_tile]
    for copy in kept:
        copy.wait()


def forward(gathered, features):
    rows, width = features.shape
    vmem = pl.BlockSpec(memory_space=pltpu.VMEM)
    hbm = pl.BlockSpec(memory_space=pltpu.HBM)
    return pl.pallas_call(
        forward_kernel,
        out_shape=(
            jax.ShapeDtypeStruct((LAYERS, rows, LANES), jnp.bfloat16),
            jax.ShapeDtypeStruct((rows, width), jnp.bfloat16),
            jax.ShapeDtypeStruct((LAYERS, rows, width), jnp.float32),
        ),
        in_specs=[hbm, vmem],
        out_specs=(vmem, vmem, hbm),
        scratch_shapes=[
            pltpu.VMEM((LAYERS, width, width), jnp.bfloat16),
            pltpu.VMEM((LAYERS, rows, width), jnp.bfloat16),
            pltpu.VMEM((LAYERS, rows, width), jnp.float32),
            pltpu.SemaphoreType.DMA((LAYERS,)),
            pltpu.SemaphoreType.DMA((LAYERS,)),
        ],
        compiler_params=pltpu.CompilerParams(vmem_limit_bytes=FORWARD_VMEM),
        cost_estimate=pl.CostEstimate(
            flops=2 * LAYERS * rows * width * width,
            bytes_accessed=LAYERS * width * (4 * width + 6 * rows),
            transcendentals=LAYERS * rows * width,
        ),
    )(gathered, features)


def backward_kernel(
    slope_ref, own_inputs_ref, slopes_in, gathered, kept_ref, given_ref,
    held, slopes, slots, sems,
):
    def factor(layer):
        below = layer - 1
        return pltpu.make_async_copy(slopes_in.at[below], slopes.at[below], sems.at[1, below])

    def start(layer):
        fetch(gathered, layer, held, layer - 1, sems.at[0, layer - 1])
        factor(layer).start()

    for layer in range(LAYERS - 1, 0, -1):
        start(layer)
    now = slope_ref
    for layer in range(LAYERS - 1, -1, -1):
        if layer > 0:
            later = slots.at[layer % 2]
            part = held.at[layer - 1]
            pltpu.make_async_copy(part, part, sems.at[0, layer - 1]).wait()
            factor(layer).wait()
            for first in range(0, held.shape[1], COLUMNS):
                columns = pl.ds(first, COLUMNS)
                upstream = lax.dot_general(
                    now[...],
                    held[layer - 1, columns, :],
                    (((1,), (1,)), ((), ())),
                    preferred_element_type=jnp.float32,
                )
                later[:, columns] = (upstream * slopes[layer - 1, :, columns]).astype(jnp.bfloat16)
        grads = jnp.dot(own_inputs_ref[layer], now[...], preferred_element_type=jnp.float32)
        kept_ref[layer] = grads[:UNITS]
        given_ref[layer] = grads[UNITS:]
        if layer > 0:
            now = later


def backward(slope, own_inputs, slopes, gathered):
    rows, width = slope.shape
    vmem = pl.BlockSpec(memory_space=pltpu.VMEM)
    hbm = pl.BlockSpec(memory_space=pltpu.HBM)
    return pl.pallas_call(
        backward_kernel,
        out_shape=(jax.ShapeDtypeStruct((LAYERS, UNITS, width), jnp.float32),) * 2,
        in_specs=[vmem, vmem, hbm, hbm],
        out_specs=(vmem,) * 2,
        scratch_shapes=[
            pltpu.VMEM((LAYERS - 1, width, width), jnp.bfloat16),
            pltpu.VMEM((LAYERS - 1, rows, width), jnp.float32),
            pltpu.VMEM((2, rows, width), jnp.bfloat16),
            pltpu.SemaphoreType.DMA((2, LAYERS - 1)),
        ],
        compiler_params=pltpu.CompilerParams(vmem_limit_bytes=WIDE_VMEM),
        cost_estimate=pl.CostEstimate(
            flops=2 * (LAYERS - 1) * rows * width * width,
            bytes_accessed=LAYERS * width * (2 * width + 4 * rows),
            transcendentals=0,
        ),
    )(slope, own_inputs, slopes, gathered)


def output_kernel(place_ref, activation_ref, fields_ref, weights_ref, left_ref, right_ref, partial_ref, residual_ref):
    del place_ref
    for first in range(0, weights_ref.shape[1], COLUMNS):
        columns = pl.ds(first, COLUMNS)
        predicted = jnp.dot(
            activation_ref[...], weights_ref[:, columns], preferred_element_type=jnp.float32
        )
        residual = ((predicted - fields_ref[:, columns]) / BATCH).astype(jnp.bfloat16)
        residual_ref[:, columns] = residual
        if first < CUT:
            left_ref[:, columns] = residual
        else:
            right_ref[:, first - CUT : first - CUT + COLUMNS] = residual
    for first in range(0, weights_ref.shape[0], COLUMNS):
        columns = pl.ds(first, COLUMNS)
        partial_ref[:, columns] = lax.dot_general(
            residual_ref[...],
            weights_ref[columns, :],
            (((1,), (1,)), ((), ())),
            preferred_element_type=jnp.float32,
        ).astype(partial_ref.dtype)


def output_layer(place, activation, fields, weights, kind):
    rows, width = activation.shape
    cells = fields.shape[1]
    return pl.pallas_call(
        output_kernel,
        out_shape=(
            jax.ShapeDtypeStruct((rows, CUT), jnp.bfloat16),
            jax.ShapeDtypeStruct((rows, cells - CUT), jnp.bfloat16),
            jax.ShapeDtypeStruct((rows, width), kind),
        ),
        grid_spec=pltpu.PrefetchScalarGridSpec(
            num_scalar_prefetch=1,
            grid=(1,),
            in_specs=[
                pl.BlockSpec((rows, width), lambda i, place: (0, 0)),
                pl.BlockSpec((rows, cells), lambda i, place: (place[0], 0)),
                pl.BlockSpec((width, cells), lambda i, place: (0, 0)),
            ],
            out_specs=(
                pl.BlockSpec((rows, CUT), lambda i, place: (0, 0)),
                pl.BlockSpec((rows, cells - CUT), lambda i, place: (0, 0)),
                pl.BlockSpec((rows, width), lambda i, place: (0, 0)),
            ),
            scratch_shapes=[pltpu.VMEM((rows, cells), jnp.bfloat16)],
        ),
        compiler_params=pltpu.CompilerParams(vmem_limit_bytes=VMEM_BYTES),
        cost_estimate=pl.CostEstimate(
            flops=4 * rows * width * cells,
            bytes_accessed=2 * width * cells + 12 * rows * cells,
            transcendentals=0,
        ),
    )(place, activation, fields, weights)


def update_kernel(
    solver_ref, own_ref, upper_ref, lower_ref, last_ref, other_last_ref, here_ref, far_ref, begun, next_ref, residual
):
    del begun
    solver_side = solver_ref[0] == 1
    step = pl.program_id(0)
    upper = step < pl.num_programs(0) // 2
    half = last_ref.shape[0]

    @pl.when(jnp.logical_and(step == 0, solver_side))
    def _():
        residual[...] = far_ref[...]

    @pl.when(jnp.logical_and(step == 0, jnp.logical_not(solver_side)))
    def _():
        residual[...] = here_ref[...]

    gradient = lax.dot_general(
        last_ref[...], residual[:half], (((0,), (0,)), ((), ())), preferred_element_type=jnp.float32
    ) + lax.dot_general(
        other_last_ref[...], residual[half:], (((0,), (0,)), ((), ())), preferred_element_type=jnp.float32
    )

    def trained(other_ref):
        momentum = momentum_decay * other_ref[...].astype(jnp.float32) + gradient
        next_ref[...] = own_ref[...] - step_size * momentum

    @pl.when(solver_side)
    def _():
        next_ref[...] = momentum_decay * own_ref[...] + gradient

    @pl.when(jnp.logical_and(upper, jnp.logical_not(solver_side)))
    def _():
        trained(upper_ref)

    @pl.when(jnp.logical_not(jnp.logical_or(upper, solver_side)))
    def _():
        trained(lower_ref)


def updated(begun, solver_side, own, upper, lower, last, other_last, here, far):
    width, cells = own.shape
    size = here.shape[1]
    steps = width // BLOCK
    chunk = 0 if begun is None else 1
    skipped = 0 if lower.shape[0] == width else steps // 2
    half = last.shape[0]
    columns = pl.BlockSpec((half, BLOCK), lambda i, flag: (0, i))
    whole = pl.BlockSpec((2 * half, size), lambda i, flag: (0, 0))
    block = pl.BlockSpec((BLOCK, size), lambda i, flag: (i, chunk))
    return pl.pallas_call(
        update_kernel,
        out_shape=jax.ShapeDtypeStruct(own.shape, jnp.float32),
        grid_spec=pltpu.PrefetchScalarGridSpec(
            num_scalar_prefetch=1,
            grid=(steps,),
            in_specs=[
                block,
                pl.BlockSpec((BLOCK, size), lambda i, flag: (jnp.minimum(i, steps // 2 - 1), 0)),
                pl.BlockSpec((BLOCK, size), lambda i, flag: (jnp.maximum(i, steps // 2) - skipped, 0)),
                columns,
                columns,
                whole,
                whole,
                pl.BlockSpec(memory_space=pl.ANY),
            ],
            out_specs=block,
            scratch_shapes=[pltpu.VMEM((2 * half, size), jnp.bfloat16)],
        ),
        input_output_aliases={} if begun is None else {8: 0},
        compiler_params=pltpu.CompilerParams(
            vmem_limit_bytes=WIDE_VMEM if begun is None else VMEM_BYTES
        ),
        cost_estimate=pl.CostEstimate(
            flops=4 * half * width * size, bytes_accessed=10 * width * size, transcendentals=0
        ),
    )(
        solver_side.astype(jnp.int32)[None], own, upper, lower, last, other_last, here, far,
        own if begun is None else begun,
    )


BLOCK = 256


def body(fields_pair, velocity, growth, features, assignment, out_pair, hidden_pair):
    solver_side = lax.axis_index("role") == 0
    core = lax.axis_index("tile_3")
    chip = lax.axis_index(CHIPS)
    fields = fields_pair[0]
    own_out = out_pair[0]
    own_hidden = hidden_pair[0]
    units = own_hidden.shape[1]
    width = own_hidden.shape[2]
    half = BATCH // 2

    hidden_narrow = own_hidden.astype(jnp.bfloat16)
    first_narrow = own_out[:, :CUT].astype(jnp.bfloat16)
    upper_narrow = own_out[:BATCH, CUT:].astype(jnp.bfloat16)
    lower_narrow = own_out[BATCH:, CUT:].astype(jnp.bfloat16)
    across = from_trainers(hidden_narrow, 1)
    across_far = from_trainers(hidden_narrow, 0)
    partner_hidden = swapped(hidden_narrow, "role")
    near = jnp.where(solver_side, partner_hidden, hidden_narrow)
    far = jnp.where(solver_side, across_far, across)
    gathered = lax.all_gather(jnp.stack([near, far]), PLANE, axis=0)

    momentum = to_trainer(first_narrow)
    early, first_narrow = lax.optimization_barrier((fields, first_narrow))
    edge = jnp.concatenate(
        [early[:, -128:], jnp.broadcast_to(velocity[None, -128:], (8, 128))], axis=0
    )

    count = lax.axis_size(TILE)
    up = [(i, (i + 1) % count) for i in range(count)]
    down = [(j, i) for i, j in up]
    before = lax.ppermute(edge, TILE, up)
    after = lax.ppermute(early[:, :128], TILE, down)
    out_narrow = tied(own_out, before, after).astype(jnp.bfloat16)
    advanced = advance(fields, before, after, velocity, growth)
    carried = jnp.take(advanced.astype(jnp.bfloat16), assignment, axis=0)
    next_batch = to_trainer(carried)
    gathered, advanced, momentum, next_batch, out_narrow = lax.optimization_barrier(
        (gathered, advanced, momentum, next_batch, out_narrow)
    )
    fields_next = jnp.where(solver_side, advanced, next_batch.astype(jnp.float32))
    tiles, last, slopes = forward(
        gathered, lax.dynamic_slice_in_dim(features, core * half, half, 0)
    )
    place = core.astype(jnp.int32)[None]
    other_last = swapped(last, "tile_3")
    left, right, kept = output_layer(place, last, fields, out_narrow, jnp.float32)
    other_left, other_right, given = output_layer(
        1 - place, tied(other_last, kept), fields, out_narrow, jnp.bfloat16
    )
    arrived = swapped(given, "tile_3")
    chip_sum = (kept + arrived.astype(jnp.float32)).astype(jnp.bfloat16)
    chips = lax.axis_size(FLOOR)
    rows = half // chips
    first = lax.axis_index(FLOOR) * rows
    shares = lax.all_to_all(
        chip_sum.reshape(chips, rows, width), FLOOR, split_axis=0, concat_axis=0, tiled=True
    )
    left = jnp.concatenate([left, other_left])
    left_far = swapped(jnp.where(solver_side, upper_narrow, left), "role")
    right = jnp.concatenate([right, other_right])
    payload = jnp.where(solver_side, lower_narrow, right)
    shares, left_far, fields_next, payload = lax.optimization_barrier(
        (shares, left_far, fields_next, payload)
    )
    plane_sum = shares.astype(jnp.float32).sum(axis=0)
    across = from_trainers(plane_sum, 1)
    across_far = from_trainers(plane_sum, 0)
    upstream = jnp.where(solver_side, to_solver(plane_sum), plane_sum) + jnp.where(
        solver_side, across_far, across
    )
    own_factor = lax.dynamic_slice_in_dim(slopes[LAYERS - 1], first, rows, 0)
    own_slope = (upstream * own_factor).astype(jnp.bfloat16)
    slope = from_everyone(own_slope, FLOOR).reshape(half, width)

    tiles = tied(tiles, own_slope)
    own_inputs = jnp.concatenate(
        [
            lax.dynamic_slice_in_dim(tiles, (chip * 2 + side) * units % LANES, units, 2)
            for side in (core, 1 - core)
        ],
        axis=2,
    ).swapaxes(1, 2)
    right_far = swapped(tied(payload, own_inputs), "role")
    out_next = updated(
        None, solver_side, own_out, momentum, momentum, last, other_last, left, left_far
    )
    slope, own_inputs, out_next = lax.optimization_barrier((slope, own_inputs, out_next))
    kept, given = backward(slope, own_inputs, slopes, gathered)
    given, right_far = lax.optimization_barrier((given, right_far))
    grad_hidden = kept + swapped(given, "tile_3")

    other_hidden = partner_hidden.astype(jnp.float32)
    out_next = updated(
        out_next, solver_side, own_out, left_far, right_far, last, other_last, right, right_far
    )
    hidden_next = jnp.where(
        solver_side,
        momentum_decay * own_hidden + grad_hidden,
        own_hidden - step_size * (momentum_decay * other_hidden + grad_hidden),
    )
    return (fields_next[None], out_next[None], hidden_next[None])


def solution(mesh):
    finer = Mesh(
        mesh.devices.reshape(SIZES), ALL
    )
    in_specs = (
        P("role", None, TILE),
        P(TILE),
        P(TILE),
        P(),
        P(),
        P("role", None, TILE),
        P("role", None, TILE, None),
    )
    out_specs = (P("role", None, TILE), P("role", None, TILE), P("role", None, TILE, None))
    return jax.shard_map(body, mesh=finer, in_specs=in_specs, out_specs=out_specs, check_vma=False)
```

```python
import itertools

import jax
import jax.numpy as jnp
from jax import lax
from jax.experimental import pallas as pl
from jax.experimental.pallas import tpu as pltpu
from jax.sharding import Mesh
from jax.sharding import PartitionSpec as P

BATCH = 512
LAYERS = 5
TILE = ("tile_0", "tile_1", "tile_2", "tile_3")
PLANE = ("tile_1", "tile_2", "tile_3")
FLOOR = ("tile_1", "tile_2")
CHIPS = ("tile_0", "tile_1", "tile_2")
ALL = ("role", *TILE)

momentum_decay = 0.9
step_size = 0.1


def to_trainer(value):
    return lax.ppermute(value, "role", [(0, 1)])


def to_solver(value):
    return lax.ppermute(value, "role", [(1, 0)])


def swapped(value, axis):
    return lax.ppermute(value, axis, [(0, 1), (1, 0)])


def from_everyone(value, axes):
    copies = jnp.broadcast_to(value, (lax.axis_size(axes), *value.shape))
    return lax.all_to_all(copies, axes, split_axis=0, concat_axis=0, tiled=True)


def ordered(mine, other, place, axis):
    return jnp.where(
        place == 0, jnp.stack([mine, other], axis), jnp.stack([other, mine], axis)
    )


def advance(fields, before, after, velocity, growth):
    states = jnp.concatenate([before[:BATCH, -1:], fields, after[:, :1]], axis=1)
    speeds = jnp.concatenate([before[BATCH, -1:], velocity])
    outflow = (
        jnp.maximum(speeds, 0.0) * states[:, :-1] + jnp.minimum(speeds, 0.0) * states[:, 1:]
    )
    carried = fields - outflow[:, 1:] + outflow[:, :-1]
    return carried + growth * carried * (1.0 - carried)


def from_trainers(value, role):
    pairs = []
    for plane, *place in itertools.product(*map(range, SIZES[1:])):
        pairs.append((flat(SIZES, (1, plane, *place)), flat(SIZES, (role, 1 - plane, *place))))
    return lax.ppermute(value, ALL, pairs)


def flat(sizes, place):
    index = 0
    for size, coordinate in zip(sizes, place):
        index = index * size + coordinate
    return index


def tied(value, *others):
    return lax.optimization_barrier((value, *others))[0]


SIZES = (2, 2, 4, 4, 2)
UNITS = 16
AHEAD = 5
CUT = 512
COLUMNS = 256
LANES = 128
VMEM_BYTES = 24 * 1024 * 1024
WIDE_VMEM = 60 * 1024 * 1024
FORWARD_VMEM = 57 * 1024 * 1024


def fetch(gathered, layer, weights, to, sem):
    plane = lax.axis_index("tile_0")
    places = gathered.shape[0]

    def step(place, carry):
        for number, half in enumerate((plane, 1 - plane)):
            row = pl.multiple_of((half * places + place) * UNITS, UNITS)
            pltpu.make_async_copy(
                gathered.at[place, number, layer], weights.at[to, pl.ds(row, UNITS)], sem
            ).start()
        return carry

    lax.fori_loop(0, places, step, 0)


def forward_kernel(
    gathered, features_ref, tiles_ref, last_ref, slopes_out,
    weights, inputs, slopes, in_sems, out_sems,
):
    chip = lax.axis_index(CHIPS)
    own_tile = pl.ds(pl.multiple_of((chip * 2 * UNITS // LANES) * LANES, LANES), LANES)
    for layer in range(AHEAD):
        fetch(gathered, layer, weights, layer, in_sems.at[layer])
    inputs[0] = features_ref[...]
    kept = []
    for layer in range(LAYERS):
        part = weights.at[layer]
        pltpu.make_async_copy(part, part, in_sems.at[layer]).wait()
        if layer + AHEAD < LAYERS:
            later = layer + AHEAD
            fetch(gathered, later, weights, later, in_sems.at[later])
        for first in range(0, weights.shape[2], COLUMNS):
            columns = pl.ds(first, COLUMNS)
            total = jnp.dot(
                inputs[layer], weights[layer, :, columns], preferred_element_type=jnp.float32
            )
            logistic = 0.5 + 0.5 * jnp.tanh(0.5 * total)
            activation = total * logistic
            if layer + 1 < LAYERS:
                inputs[layer + 1, :, columns] = activation.astype(jnp.bfloat16)
            else:
                last_ref[:, columns] = activation.astype(jnp.bfloat16)
            slopes[layer, :, columns] = logistic + activation * (1.0 - logistic)
        kept.append(pltpu.make_async_copy(slopes.at[layer], slopes_out.at[layer], out_sems.at[layer]))
        kept[-1].start()
        tiles_ref[layer] = inputs[layer, :, own_tile]
    for copy in kept:
        copy.wait()


def forward(gathered, features):
    rows, width = features.shape
    vmem = pl.BlockSpec(memory_space=pltpu.VMEM)
    hbm = pl.BlockSpec(memory_space=pltpu.HBM)
    return pl.pallas_call(
        forward_kernel,
        out_shape=(
            jax.ShapeDtypeStruct((LAYERS, rows, LANES), jnp.bfloat16),
            jax.ShapeDtypeStruct((rows, width), jnp.bfloat16),
            jax.ShapeDtypeStruct((LAYERS, rows, width), jnp.float32),
        ),
        in_specs=[hbm, vmem],
        out_specs=(vmem, vmem, hbm),
        scratch_shapes=[
            pltpu.VMEM((LAYERS, width, width), jnp.bfloat16),
            pltpu.VMEM((LAYERS, rows, width), jnp.bfloat16),
            pltpu.VMEM((LAYERS, rows, width), jnp.float32),
            pltpu.SemaphoreType.DMA((LAYERS,)),
            pltpu.SemaphoreType.DMA((LAYERS,)),
        ],
        compiler_params=pltpu.CompilerParams(vmem_limit_bytes=FORWARD_VMEM),
        cost_estimate=pl.CostEstimate(
            flops=2 * LAYERS * rows * width * width,
            bytes_accessed=LAYERS * width * (4 * width + 6 * rows),
            transcendentals=LAYERS * rows * width,
        ),
    )(gathered, features)


def backward_kernel(
    slope_ref, own_inputs_ref, slopes_in, gathered, kept_ref, given_ref,
    held, slopes, slots, sems,
):
    def factor(layer):
        below = layer - 1
        return pltpu.make_async_copy(slopes_in.at[below], slopes.at[below], sems.at[1, below])

    def start(layer):
        fetch(gathered, layer, held, layer - 1, sems.at[0, layer - 1])
        factor(layer).start()

    for layer in range(LAYERS - 1, 0, -1):
        start(layer)
    now = slope_ref
    for layer in range(LAYERS - 1, -1, -1):
        if layer > 0:
            later = slots.at[layer % 2]
            part = held.at[layer - 1]
            pltpu.make_async_copy(part, part, sems.at[0, layer - 1]).wait()
            factor(layer).wait()
            for first in range(0, held.shape[1], COLUMNS):
                columns = pl.ds(first, COLUMNS)
                upstream = lax.dot_general(
                    now[...],
                    held[layer - 1, columns, :],
                    (((1,), (1,)), ((), ())),
                    preferred_element_type=jnp.float32,
                )
                later[:, columns] = (upstream * slopes[layer - 1, :, columns]).astype(jnp.bfloat16)
        grads = jnp.dot(own_inputs_ref[layer], now[...], preferred_element_type=jnp.float32)
        kept_ref[layer] = grads[:UNITS]
        given_ref[layer] = grads[UNITS:]
        if layer > 0:
            now = later


def backward(slope, own_inputs, slopes, gathered):
    rows, width = slope.shape
    vmem = pl.BlockSpec(memory_space=pltpu.VMEM)
    hbm = pl.BlockSpec(memory_space=pltpu.HBM)
    return pl.pallas_call(
        backward_kernel,
        out_shape=(jax.ShapeDtypeStruct((LAYERS, UNITS, width), jnp.float32),) * 2,
        in_specs=[vmem, vmem, hbm, hbm],
        out_specs=(vmem,) * 2,
        scratch_shapes=[
            pltpu.VMEM((LAYERS - 1, width, width), jnp.bfloat16),
            pltpu.VMEM((LAYERS - 1, rows, width), jnp.float32),
            pltpu.VMEM((2, rows, width), jnp.bfloat16),
            pltpu.SemaphoreType.DMA((2, LAYERS - 1)),
        ],
        compiler_params=pltpu.CompilerParams(vmem_limit_bytes=WIDE_VMEM),
        cost_estimate=pl.CostEstimate(
            flops=2 * (LAYERS - 1) * rows * width * width,
            bytes_accessed=LAYERS * width * (2 * width + 4 * rows),
            transcendentals=0,
        ),
    )(slope, own_inputs, slopes, gathered)


def output_kernel(place_ref, activation_ref, fields_ref, weights_ref, left_ref, right_ref, partial_ref, residual_ref):
    del place_ref
    for first in range(0, weights_ref.shape[1], COLUMNS):
        columns = pl.ds(first, COLUMNS)
        predicted = jnp.dot(
            activation_ref[...], weights_ref[:, columns], preferred_element_type=jnp.float32
        )
        residual = ((predicted - fields_ref[:, columns]) / BATCH).astype(jnp.bfloat16)
        residual_ref[:, columns] = residual
        if first < CUT:
            left_ref[:, columns] = residual
        else:
            right_ref[:, first - CUT : first - CUT + COLUMNS] = residual
    for first in range(0, weights_ref.shape[0], COLUMNS):
        columns = pl.ds(first, COLUMNS)
        partial_ref[:, columns] = lax.dot_general(
            residual_ref[...],
            weights_ref[columns, :],
            (((1,), (1,)), ((), ())),
            preferred_element_type=jnp.float32,
        ).astype(partial_ref.dtype)


def output_layer(place, activation, fields, weights, kind):
    rows, width = activation.shape
    cells = fields.shape[1]
    return pl.pallas_call(
        output_kernel,
        out_shape=(
            jax.ShapeDtypeStruct((rows, CUT), jnp.bfloat16),
            jax.ShapeDtypeStruct((rows, cells - CUT), jnp.bfloat16),
            jax.ShapeDtypeStruct((rows, width), kind),
        ),
        grid_spec=pltpu.PrefetchScalarGridSpec(
            num_scalar_prefetch=1,
            grid=(1,),
            in_specs=[
                pl.BlockSpec((rows, width), lambda i, place: (0, 0)),
                pl.BlockSpec((rows, cells), lambda i, place: (place[0], 0)),
                pl.BlockSpec((width, cells), lambda i, place: (0, 0)),
            ],
            out_specs=(
                pl.BlockSpec((rows, CUT), lambda i, place: (0, 0)),
                pl.BlockSpec((rows, cells - CUT), lambda i, place: (0, 0)),
                pl.BlockSpec((rows, width), lambda i, place: (0, 0)),
            ),
            scratch_shapes=[pltpu.VMEM((rows, cells), jnp.bfloat16)],
        ),
        compiler_params=pltpu.CompilerParams(vmem_limit_bytes=VMEM_BYTES),
        cost_estimate=pl.CostEstimate(
            flops=4 * rows * width * cells,
            bytes_accessed=2 * width * cells + 12 * rows * cells,
            transcendentals=0,
        ),
    )(place, activation, fields, weights)


def update_kernel(
    solver_ref, own_ref, upper_ref, lower_ref, last_ref, other_last_ref, here_ref, far_ref, begun, next_ref, residual
):
    del begun
    solver_side = solver_ref[0] == 1
    step = pl.program_id(0)
    upper = step < pl.num_programs(0) // 2
    half = last_ref.shape[0]

    @pl.when(jnp.logical_and(step == 0, solver_side))
    def _():
        residual[...] = far_ref[...]

    @pl.when(jnp.logical_and(step == 0, jnp.logical_not(solver_side)))
    def _():
        residual[...] = here_ref[...]

    gradient = lax.dot_general(
        last_ref[...], residual[:half], (((0,), (0,)), ((), ())), preferred_element_type=jnp.float32
    ) + lax.dot_general(
        other_last_ref[...], residual[half:], (((0,), (0,)), ((), ())), preferred_element_type=jnp.float32
    )

    def trained(other_ref):
        momentum = momentum_decay * other_ref[...].astype(jnp.float32) + gradient
        next_ref[...] = own_ref[...] - step_size * momentum

    @pl.when(solver_side)
    def _():
        next_ref[...] = momentum_decay * own_ref[...] + gradient

    @pl.when(jnp.logical_and(upper, jnp.logical_not(solver_side)))
    def _():
        trained(upper_ref)

    @pl.when(jnp.logical_not(jnp.logical_or(upper, solver_side)))
    def _():
        trained(lower_ref)


def updated(begun, solver_side, own, upper, lower, last, other_last, here, far):
    width, cells = own.shape
    size = here.shape[1]
    steps = width // BLOCK
    chunk = 0 if begun is None else 1
    skipped = 0 if lower.shape[0] == width else steps // 2
    half = last.shape[0]
    columns = pl.BlockSpec((half, BLOCK), lambda i, flag: (0, i))
    whole = pl.BlockSpec((2 * half, size), lambda i, flag: (0, 0))
    block = pl.BlockSpec((BLOCK, size), lambda i, flag: (i, chunk))
    return pl.pallas_call(
        update_kernel,
        out_shape=jax.ShapeDtypeStruct(own.shape, jnp.float32),
        grid_spec=pltpu.PrefetchScalarGridSpec(
            num_scalar_prefetch=1,
            grid=(steps,),
            in_specs=[
                block,
                pl.BlockSpec((BLOCK, size), lambda i, flag: (jnp.minimum(i, steps // 2 - 1), 0)),
                pl.BlockSpec((BLOCK, size), lambda i, flag: (jnp.maximum(i, steps // 2) - skipped, 0)),
                columns,
                columns,
                whole,
                whole,
                pl.BlockSpec(memory_space=pl.ANY),
            ],
            out_specs=block,
            scratch_shapes=[pltpu.VMEM((2 * half, size), jnp.bfloat16)],
        ),
        input_output_aliases={} if begun is None else {8: 0},
        compiler_params=pltpu.CompilerParams(
            vmem_limit_bytes=WIDE_VMEM if begun is None else VMEM_BYTES
        ),
        cost_estimate=pl.CostEstimate(
            flops=4 * half * width * size, bytes_accessed=10 * width * size, transcendentals=0
        ),
    )(
        solver_side.astype(jnp.int32)[None], own, upper, lower, last, other_last, here, far,
        own if begun is None else begun,
    )


BLOCK = 512


def body(fields_pair, velocity, growth, features, assignment, out_pair, hidden_pair):
    solver_side = lax.axis_index("role") == 0
    core = lax.axis_index("tile_3")
    chip = lax.axis_index(CHIPS)
    fields = fields_pair[0]
    own_out = out_pair[0]
    own_hidden = hidden_pair[0]
    units = own_hidden.shape[1]
    width = own_hidden.shape[2]
    half = BATCH // 2

    hidden_narrow = own_hidden.astype(jnp.bfloat16)
    first_narrow = own_out[:, :CUT].astype(jnp.bfloat16)
    upper_narrow = own_out[:BATCH, CUT:].astype(jnp.bfloat16)
    lower_narrow = own_out[BATCH:, CUT:].astype(jnp.bfloat16)
    across = from_trainers(hidden_narrow, 1)
    across_far = from_trainers(hidden_narrow, 0)
    partner_hidden = swapped(hidden_narrow, "role")
    near = jnp.where(solver_side, partner_hidden, hidden_narrow)
    far = jnp.where(solver_side, across_far, across)
    gathered = lax.all_gather(jnp.stack([near, far]), PLANE, axis=0)

    momentum = to_trainer(first_narrow)
    early, first_narrow = lax.optimization_barrier((fields, first_narrow))
    edge = jnp.concatenate(
        [early[:, -128:], jnp.broadcast_to(velocity[None, -128:], (8, 128))], axis=0
    )

    count = lax.axis_size(TILE)
    up = [(i, (i + 1) % count) for i in range(count)]
    down = [(j, i) for i, j in up]
    before = lax.ppermute(edge, TILE, up)
    after = lax.ppermute(early[:, :128], TILE, down)
    out_narrow = tied(own_out, before, after).astype(jnp.bfloat16)
    advanced = advance(fields, before, after, velocity, growth)
    carried = jnp.take(advanced.astype(jnp.bfloat16), assignment, axis=0)
    next_batch = to_trainer(carried)
    gathered, advanced, momentum, next_batch, out_narrow = lax.optimization_barrier(
        (gathered, advanced, momentum, next_batch, out_narrow)
    )
    fields_next = jnp.where(solver_side, advanced, next_batch.astype(jnp.float32))
    tiles, last, slopes = forward(
        gathered, lax.dynamic_slice_in_dim(features, core * half, half, 0)
    )
    place = core.astype(jnp.int32)[None]
    other_last = swapped(last, "tile_3")
    left, right, kept = output_layer(place, last, fields, out_narrow, jnp.float32)
    other_left, other_right, given = output_layer(
        1 - place, tied(other_last, kept), fields, out_narrow, jnp.bfloat16
    )
    arrived = swapped(given, "tile_3")
    chip_sum = (kept + arrived.astype(jnp.float32)).astype(jnp.bfloat16)
    chips = lax.axis_size(FLOOR)
    rows = half // chips
    first = lax.axis_index(FLOOR) * rows
    shares = lax.all_to_all(
        chip_sum.reshape(chips, rows, width), FLOOR, split_axis=0, concat_axis=0, tiled=True
    )
    left = jnp.concatenate([left, other_left])
    left_far = swapped(jnp.where(solver_side, upper_narrow, left), "role")
    right = jnp.concatenate([right, other_right])
    payload = jnp.where(solver_side, lower_narrow, right)
    shares, left_far, fields_next, payload = lax.optimization_barrier(
        (shares, left_far, fields_next, payload)
    )
    plane_sum = shares.astype(jnp.float32).sum(axis=0)
    straight = to_solver(plane_sum)
    across_far = from_trainers(plane_sum, 0)
    across = from_trainers(plane_sum, 1)
    upstream = jnp.where(solver_side, straight, plane_sum) + jnp.where(solver_side, across_far, across)
    own_factor = lax.dynamic_slice_in_dim(slopes[LAYERS - 1], first, rows, 0)
    own_slope = (upstream * own_factor).astype(jnp.bfloat16)
    slope = from_everyone(own_slope, FLOOR).reshape(half, width)

    tiles = tied(tiles, own_slope)
    own_inputs = jnp.concatenate(
        [
            lax.dynamic_slice_in_dim(tiles, (chip * 2 + side) * units % LANES, units, 2)
            for side in (core, 1 - core)
        ],
        axis=2,
    ).swapaxes(1, 2)
    right_far = swapped(tied(payload, own_inputs), "role")
    out_next = updated(
        None, solver_side, own_out, momentum, momentum, last, other_last, left, left_far
    )
    slope, own_inputs, out_next = lax.optimization_barrier((slope, own_inputs, out_next))
    kept, given = backward(slope, own_inputs, slopes, gathered)
    given, right_far = lax.optimization_barrier((given, right_far))
    grad_hidden = kept + swapped(given, "tile_3")

    other_hidden = partner_hidden.astype(jnp.float32)
    out_next = updated(
        out_next, solver_side, own_out, left_far, right_far, last, other_last, right, right_far
    )
    hidden_next = jnp.where(
        solver_side,
        momentum_decay * own_hidden + grad_hidden,
        own_hidden - step_size * (momentum_decay * other_hidden + grad_hidden),
    )
    return (fields_next[None], out_next[None], hidden_next[None])


def solution(mesh):
    finer = Mesh(
        mesh.devices.reshape(SIZES), ALL
    )
    in_specs = (
        P("role", None, TILE),
        P(TILE),
        P(TILE),
        P(),
        P(),
        P("role", None, TILE),
        P("role", None, TILE, None),
    )
    out_specs = (P("role", None, TILE), P("role", None, TILE), P("role", None, TILE, None))
    return jax.shard_map(body, mesh=finer, in_specs=in_specs, out_specs=out_specs, check_vma=False)
```
